32 devices in a mesh: groups: 2 (over y), tile: 4 (over z), depth: 2 (over x), rep: 2 (over core).
Axes of the slice: x: 2, y: 2, z: 4, core: 2. Of those that a mesh axis runs over, the one named last changes fastest.
Arguments:
- cycle_integrals: float32 [10240, 32000], P(('groups', 'depth', 'rep'), 'tile'), parts along dimension 0, may hold values from -0.09375 to 0.09375
- amplitudes: float32 [5120, 32000], P('groups', 'tile'), parts along dimension 0, may hold values from -6 to 6
- occupied_irreps: int32 [160], P('groups'), parts along dimension 0, may hold values from 0 to 7
- virtual_irreps: int32 [1600], P('groups'), parts along dimension 0, may hold values from 0 to 7
Outputs:
- cycle_residual: float32 [5120, 5120], P(('groups', 'tile'), ('depth', 'rep')), parts along dimension 0
The draws below stay inside these ranges and needn't reach their ends.
There are 2 independent parts, one for each index of `groups`. The reference program is written for one: setup_inputs(seed, part) draws one part's arguments, and reference() takes and returns one part's arrays. A program takes and returns all parts, laid end to end along the dimension named above; each array names one. Nothing has to cross between parts.
Inputs may be any that keep to these rules, and one draw needn't show every extreme that they name: `occupied_irreps`: D2h irrep labels; the product of two irreps is their exclusive or. `virtual_irreps`: D2h irrep labels; the product of two irreps is their exclusive or.
All inputs are finite; a program needn't handle non-finite values.
Results may differ from the reference program's by a relative error of at most 0.000071.
Values sent between devices are 32-bit elements; how exact they have to be, the bound alone decides.
A program may use at most 320 MiB of HBM per device.

```python
import math
import jax
import jax.numpy as jnp
import numpy as np
from jax import lax

OCC = 80
VIRT = 800
CW = 400
AI = 5120
BJ = 2560
CK = 32000


def plant(result, stream_key, smallest, high):
    spot = [jax.random.randint(jax.random.fold_in(stream_key, axis), (), 0, length) for axis, length in enumerate(result.shape)]
    widest = result.shape.index(max(result.shape))
    neighbour = spot[:widest] + [(spot[widest] + 1) % result.shape[widest]] + spot[widest + 1:]
    return result.at[tuple(spot)].set(smallest).at[tuple(neighbour)].set(high)


def block_scale(rng, dims, pieces, smallest, top_value):
    gain, own = 1.0, jax.random.fold_in(rng, 6)
    for dim, blocks in pieces:
        steps = jnp.exp(jax.random.uniform(jax.random.fold_in(own, dim), (blocks,), jnp.float32, smallest / len(pieces), top_value / len(pieces)))
        gain = gain * jnp.repeat(steps, dims[dim] // blocks).reshape([-1 if axis == dim else 1 for axis in range(len(dims))])
    return gain


def rank_bounds(count, lean):
    weights = [(1 << 20) // math.isqrt(standing ** lean) + 1 for standing in range(1, count + 1)]
    spread = 1 + sum(weights) // (1 << 30)
    return np.cumsum(np.array([max(1, weight // spread) for weight in weights]))


def ranked_ids(key, extent, number_of, lean):
    table = rank_bounds(number_of, lean)
    ticket = jax.random.randint(jax.random.fold_in(key, 1), extent, 0, int(table[number_of - 1]))
    standing = jnp.searchsorted(jnp.asarray(table, jnp.int32), ticket, side="right")
    return jax.random.permutation(jax.random.fold_in(key, 2), number_of)[standing].astype(jnp.int32)


def scatter_about(stream_key, shape, deviation, bound, pieces=(), kind=jnp.bfloat16):
    drawn = deviation * jax.random.normal(stream_key, shape, jnp.float32)
    if pieces:
        drawn = drawn * block_scale(stream_key, shape, pieces, -0.22, 0.18)
    return jnp.clip(drawn, -bound, bound).astype(kind)


def setup_inputs(seed: int = 0, part: int = 0) -> dict:
    keys = jax.random.split(jax.random.key(seed), 5)
    part_splits = jax.random.split(jax.random.fold_in(keys[4], part), 5)
    cycle_integrals = scatter_about(part_splits[0], (AI, CK), (CW * OCC // 8) ** -0.5, 0.09375, ((0, 4), (1, 4)), jnp.float32)
    amplitudes = scatter_about(part_splits[1], (BJ, CK), 1.0, 6.0, ((1, 4),), jnp.float32)
    occupied_irreps = plant(ranked_ids(part_splits[2], (OCC,), 8, 2), jax.random.fold_in(part_splits[2], 3), 0, 7).astype(jnp.int32)
    virtual_irreps = plant(ranked_ids(part_splits[3], (VIRT,), 8, 2), jax.random.fold_in(part_splits[3], 3), 0, 7).astype(jnp.int32)
    return dict(cycle_integrals=cycle_integrals, amplitudes=amplitudes, occupied_irreps=occupied_irreps, virtual_irreps=virtual_irreps)


def reference(cycle_integrals, amplitudes, occupied_irreps, virtual_irreps):
    pair_irreps = jnp.bitwise_xor(virtual_irreps[:, None], occupied_irreps[None, :]).reshape(-1)
    row_count = cycle_integrals.shape[0]
    column_count = amplitudes.shape[0]
    depth_count = cycle_integrals.shape[1]
    contracted = pair_irreps[:depth_count]
    integrals = jnp.where(pair_irreps[:row_count][:, None] == contracted[None, :], cycle_integrals, jnp.zeros((), cycle_integrals.dtype))
    masked_amplitudes = jnp.where(pair_irreps[:column_count][:, None] == contracted[None, :], amplitudes, jnp.zeros((), amplitudes.dtype))
    return lax.dot_general(masked_amplitudes, integrals, (((1,), (1,)), ((), ())), precision=lax.Precision.HIGHEST, preferred_element_type=jnp.float32)
```

```python
import functools

import jax
import jax.numpy as jnp
from jax import lax
from jax.experimental import pallas as pl
from jax.experimental.pallas import tpu as pltpu
from jax.sharding import PartitionSpec as P

BF16, F32 = jnp.bfloat16, jnp.float32
DEPTH_BLOCK = 512


def split(x):
    high = x.astype(BF16)
    return high, (x - high.astype(F32)).astype(BF16)


def contract_kernel(slots, row_tile, rank_ref, arow_ref, irow_ref, col_ref, a_ref, i_ref, z_ref, pick_ref, y_ref):
    step = pl.program_id(0)

    @pl.when(step == 0)
    def _():
        slot = lax.broadcasted_iota(jnp.int32, pick_ref.shape, 0)
        pick_ref[...] = jnp.where(slot == rank_ref[...], 1.0, 0.0).astype(BF16)
        z_ref[...] = jnp.zeros_like(z_ref)

    cols = col_ref[...]
    high, low = split(jnp.where(irow_ref[...] == cols, i_ref[...], 0.0))
    y_ref[:slots] = jnp.dot(pick_ref[...], high, preferred_element_type=F32).astype(BF16)
    y_ref[slots:] = jnp.dot(pick_ref[...], low, preferred_element_type=F32).astype(BF16)

    def rows(t, carry):
        here = pl.ds(pl.multiple_of(t * row_tile, row_tile), row_tile)
        a_high, a_low = split(jnp.where(arow_ref[here, :] == cols, a_ref[here, :], 0.0))
        nt = (((1,), (1,)), ((), ()))
        both = lax.dot_general(a_high, y_ref[...], nt, preferred_element_type=F32)
        rest = lax.dot_general(a_low, y_ref[:slots], nt, preferred_element_type=F32)
        z_ref[here, :] += both[:, :slots] + both[:, slots:] + rest
        return carry

    lax.fori_loop(0, a_ref.shape[0] // row_tile, rows, 0)


def contract(amplitudes, integrals, rank, arows, irows, cols, slots):
    m, depth = amplitudes.shape
    n = integrals.shape[0]
    kb = DEPTH_BLOCK
    steps = pl.cdiv(depth, kb)
    row_tile = 512 if m % 512 == 0 else m
    cols = jnp.pad(cols, (0, steps * kb - depth), constant_values=-1)
    whole = lambda s: (0, 0)
    return pl.pallas_call(
        functools.partial(contract_kernel, slots, row_tile),
        grid=(steps,),
        out_shape=jax.ShapeDtypeStruct((m, slots), F32),
        in_specs=[
            pl.BlockSpec((1, n), whole),
            pl.BlockSpec((m, 1), whole),
            pl.BlockSpec((n, 1), whole),
            pl.BlockSpec((1, kb), lambda s: (0, s)),
            pl.BlockSpec((m, kb), lambda s: (0, s)),
            pl.BlockSpec((n, kb), lambda s: (0, s)),
        ],
        out_specs=pl.BlockSpec((m, slots), whole),
        scratch_shapes=[pltpu.VMEM((slots, n), BF16), pltpu.VMEM((2 * slots, kb), BF16)],
        compiler_params=pltpu.CompilerParams(vmem_limit_bytes=52 * 1024 * 1024),
        cost_estimate=pl.CostEstimate(
            flops=2 * m * slots * depth * 3 + 4 * n * slots * depth,
            bytes_accessed=4 * (m + n) * depth + 4 * m * slots,
            transcendentals=0,
        ),
    )(rank[None, :], arows[:, None], irows[:, None], cols[None, :], amplitudes, integrals)


def expand_kernel(slots, rank_ref, icol_ref, row_ref, z_ref, out_ref):
    slot = lax.broadcasted_iota(jnp.int32, (slots, rank_ref.shape[1]), 0)
    pick = jnp.where(slot == rank_ref[...], 1.0, 0.0).astype(BF16)
    high, low = split(z_ref[...])
    full = jnp.dot(high, pick, preferred_element_type=F32) + jnp.dot(low, pick, preferred_element_type=F32)
    out_ref[...] = jnp.where(row_ref[...] == icol_ref[...], full, 0.0)


def expand(z, rank, irows, kept):
    m, slots = z.shape
    n = rank.shape[0]
    block = m // 4 if m % 64 == 0 else m
    whole = lambda s: (0, 0)
    return pl.pallas_call(
        functools.partial(expand_kernel, slots),
        grid=(m // block,),
        out_shape=jax.ShapeDtypeStruct((m, n), F32),
        in_specs=[
            pl.BlockSpec((1, n), whole),
            pl.BlockSpec((1, n), whole),
            pl.BlockSpec((block, 1), lambda s: (s, 0)),
            pl.BlockSpec((block, slots), lambda s: (s, 0)),
        ],
        out_specs=pl.BlockSpec((block, n), lambda s: (s, 0)),
        compiler_params=pltpu.CompilerParams(vmem_limit_bytes=32 * 1024 * 1024),
    )(rank[None, :], irows[None, :], kept[:, None], z)


def local(cycle_integrals, amplitudes, occupied_irreps, virtual_irreps):
    n, depth = cycle_integrals.shape
    m = amplitudes.shape[0]
    tiles = lax.axis_size("tile")
    occ = occupied_irreps.shape[0]
    reps = lax.axis_size("depth") * lax.axis_size("rep")
    used = -(-max(tiles * depth, m, reps * n) // occ)
    pair_irreps = jnp.bitwise_xor(virtual_irreps[:used, None], occupied_irreps[None, :]).reshape(-1)
    cols = lax.dynamic_slice_in_dim(pair_irreps, lax.axis_index("tile") * depth, depth)
    row_start = (lax.axis_index("depth") * lax.axis_size("rep") + lax.axis_index("rep")) * n
    irows = lax.dynamic_slice_in_dim(pair_irreps, row_start, n)
    arows = pair_irreps[:m]
    kept_rows = m // tiles
    kept = lax.dynamic_slice_in_dim(arows, lax.axis_index("tile") * kept_rows, kept_rows)

    at = jnp.arange(n, dtype=jnp.int32)
    earlier = (irows[:, None] == irows[None, :]) & (at[:, None] < at[None, :])
    rank = jnp.sum(earlier.astype(jnp.int32), axis=0)
    slots = -(-3 * n // 1280) * 128
    rounds = lax.pmax(jnp.max(rank) // slots + 1, ("groups", "tile", "depth", "rep"))

    def one_round(base):
        moved = rank - base
        z = contract(amplitudes, cycle_integrals, moved, arows, irows, cols, slots)
        z = lax.psum_scatter(z, "tile", scatter_dimension=0, tiled=True)
        return expand(z, moved, irows, kept)

    out = one_round(0)

    def more(state):
        r, total = state
        return r + 1, total + one_round(r * slots)

    return lax.while_loop(lambda s: s[0] < rounds, more, (jnp.int32(1), out))[1]


def solution(mesh):
    return jax.shard_map(
        local,
        mesh=mesh,
        in_specs=(
            P(("groups", "depth", "rep"), "tile"),
            P("groups", "tile"),
            P("groups"),
            P("groups"),
        ),
        out_specs=P(("groups", "tile"), ("depth", "rep")),
        check_vma=False,
    )
```

```python
import functools

import jax
import jax.numpy as jnp
from jax import lax
from jax.experimental import pallas as pl
from jax.experimental.pallas import tpu as pltpu
from jax.sharding import PartitionSpec as P

BF16, F32 = jnp.bfloat16, jnp.float32
def split(x):
    high = x.astype(BF16)
    return high, (x - high.astype(F32)).astype(BF16)


def merge_kernel(slots, rank_ref, irow_ref, col_ref, i_ref, y_ref, pick_ref):
    @pl.when(pl.program_id(0) == 0)
    def _():
        slot = lax.broadcasted_iota(jnp.int32, pick_ref.shape, 0)
        pick_ref[...] = jnp.where(slot == rank_ref[...], 1.0, 0.0).astype(BF16)

    high, low = split(jnp.where(irow_ref[...] == col_ref[...], i_ref[...], 0.0))
    nt = (((1,), (1,)), ((), ()))
    y_ref[:slots] = lax.dot_general(pick_ref[...], high, nt, preferred_element_type=F32).astype(BF16)
    y_ref[slots:] = lax.dot_general(pick_ref[...], low, nt, preferred_element_type=F32).astype(BF16)


def merge(integrals_t, rank, irows, cols, slots):
    depth, n = integrals_t.shape
    kb = 512
    padded = cols.shape[0]
    whole = lambda s: (0, 0)
    return pl.pallas_call(
        functools.partial(merge_kernel, slots),
        grid=(padded // kb,),
        out_shape=jax.ShapeDtypeStruct((2 * slots, padded), BF16),
        in_specs=[
            pl.BlockSpec((1, n), whole),
            pl.BlockSpec((1, n), whole),
            pl.BlockSpec((kb, 1), lambda s: (s, 0)),
            pl.BlockSpec((kb, n), lambda s: (jnp.minimum(s, (depth - 1) // kb), 0)),
        ],
        out_specs=pl.BlockSpec((2 * slots, kb), lambda s: (0, s)),
        scratch_shapes=[pltpu.VMEM((slots, n), BF16)],
        compiler_params=pltpu.CompilerParams(vmem_limit_bytes=40 * 1024 * 1024),
        cost_estimate=pl.CostEstimate(
            flops=4 * n * slots * depth, bytes_accessed=4 * (n + slots) * depth, transcendentals=0
        ),
    )(rank[None, :], irows[None, :], cols[:, None], integrals_t)


def chunk_kernel(slots, dest_ref, arow_ref, col_ref, a_ref, y_ref, z_ref):
    @pl.when(pl.program_id(0) == 0)
    def _():
        z_ref[...] = jnp.zeros_like(z_ref)

    a_high, a_low = split(jnp.where(arow_ref[...] == col_ref[...], a_ref[...], 0.0))
    both = jnp.dot(y_ref[...], a_high, preferred_element_type=F32)
    rest = jnp.dot(y_ref[:slots], a_low, preferred_element_type=F32)
    z_ref[...] += both[:slots] + both[slots:] + rest


def chunk(dest, amplitudes_t, y, arows, cols, width):
    depth, m = amplitudes_t.shape
    slots = y.shape[0] // 2
    kb = 1024 if width <= 1280 else 512
    return pl.pallas_call(
        functools.partial(chunk_kernel, slots),
        grid_spec=pltpu.PrefetchScalarGridSpec(
            num_scalar_prefetch=1,
            grid=(pl.cdiv(depth, kb),),
            in_specs=[
                pl.BlockSpec((1, width), lambda s, d: (0, d[0])),
                pl.BlockSpec((kb, 1), lambda s, d: (s, 0)),
                pl.BlockSpec((kb, width), lambda s, d: (s, d[0])),
                pl.BlockSpec((2 * slots, kb), lambda s, d: (0, s)),
            ],
            out_specs=pl.BlockSpec((slots, width), lambda s, d: (0, 0)),
        ),
        out_shape=jax.ShapeDtypeStruct((slots, width), F32),
        compiler_params=pltpu.CompilerParams(vmem_limit_bytes=52 * 1024 * 1024),
        cost_estimate=pl.CostEstimate(
            flops=6 * width * slots * depth, bytes_accessed=4 * (width + slots) * depth, transcendentals=0
        ),
    )(dest, arows[None, :], cols[:, None], amplitudes_t, y)


def expand_kernel(slots, rank_ref, icol_ref, row_ref, *refs):
    out_ref = refs[-1]
    slot = lax.broadcasted_iota(jnp.int32, (slots, rank_ref.shape[1]), 0)
    pick = jnp.where(slot == rank_ref[...], 1.0, 0.0).astype(BF16)
    total = refs[0][...]
    for z_ref in refs[1:-1]:
        total += z_ref[...]
    high, low = split(total.T)
    full = jnp.dot(high, pick, preferred_element_type=F32) + jnp.dot(low, pick, preferred_element_type=F32)
    out_ref[...] = jnp.where(row_ref[...] == icol_ref[...], full, 0.0)


def expand(terms, rank, irows, kept):
    slots, m = terms[0].shape
    n = rank.shape[0]
    block = 128 if m % 128 == 0 else m
    whole = lambda s: (0, 0)
    return pl.pallas_call(
        functools.partial(expand_kernel, slots),
        grid=(m // block,),
        out_shape=jax.ShapeDtypeStruct((m, n), F32),
        in_specs=[
            pl.BlockSpec((1, n), whole),
            pl.BlockSpec((1, n), whole),
            pl.BlockSpec((block, 1), lambda s: (s, 0)),
        ]
        + [pl.BlockSpec((slots, block), lambda s: (0, s))] * len(terms),
        out_specs=pl.BlockSpec((block, n), lambda s: (s, 0)),
        compiler_params=pltpu.CompilerParams(vmem_limit_bytes=32 * 1024 * 1024),
    )(rank[None, :], irows[None, :], kept[:, None], *terms)


def local(cycle_integrals, amplitudes, occupied_irreps, virtual_irreps):
    n, depth = cycle_integrals.shape
    m = amplitudes.shape[0]
    tiles = lax.axis_size("tile")
    occ = occupied_irreps.shape[0]
    reps = lax.axis_size("depth") * lax.axis_size("rep")
    used = -(-max(tiles * depth, m, reps * n) // occ)
    pair_irreps = jnp.bitwise_xor(virtual_irreps[:used, None], occupied_irreps[None, :]).reshape(-1)
    me = lax.axis_index("tile")
    cols = lax.dynamic_slice_in_dim(pair_irreps, me * depth, depth)
    cols = jnp.pad(cols, (0, -depth % 1024), constant_values=-1)
    row_start = (lax.axis_index("depth") * lax.axis_size("rep") + lax.axis_index("rep")) * n
    irows = lax.dynamic_slice_in_dim(pair_irreps, row_start, n)
    arows = pair_irreps[:m]
    kept_rows = m // tiles
    kept = lax.dynamic_slice_in_dim(arows, me * kept_rows, kept_rows)

    at = jnp.arange(n, dtype=jnp.int32)
    earlier = (irows[:, None] == irows[None, :]) & (at[:, None] < at[None, :])
    rank = jnp.sum(earlier.astype(jnp.int32), axis=0)
    slots = -(-3 * n // 1280) * 128

    every = pair_irreps[: reps * n].reshape(1, reps, n)
    counts = jnp.sum((every == jnp.arange(8, dtype=jnp.int32)[:, None, None]).astype(jnp.int32), axis=2)
    mine = jnp.broadcast_to(jnp.max(counts), (8, 128))
    most = mine
    groups = lax.axis_size("groups")
    for shift in range(1, groups):
        other = lax.ppermute(mine, "groups", [(g, (g + shift) % groups) for g in range(groups)])
        most = jnp.maximum(most, other)
    rounds = (most[0, 0] + slots - 1) // slots

    integrals_t, amplitudes_t = cycle_integrals.T, amplitudes.T

    def one_round(base):
        moved = rank - base
        y = merge(integrals_t, moved, irows, cols, slots)
        if tiles > 4 or kept_rows % 128:
            z = chunk(jnp.zeros((1,), jnp.int32), amplitudes_t, y, arows, cols, m)
            terms = [lax.psum_scatter(z, "tile", scatter_dimension=1, tiled=True)]
        else:
            terms, last = [], None
            far = sorted(range(1, tiles), key=lambda s: abs(2 * s - tiles))
            for shift in far + [0]:
                dest = lax.rem(me + shift, tiles).astype(jnp.int32).reshape(1)
                if last is not None:
                    dest, _ = lax.optimization_barrier((dest, last))
                last = chunk(dest, amplitudes_t, y, arows, cols, kept_rows)
                if shift:
                    terms.append(lax.ppermute(last, "tile", [(t, (t + shift) % tiles) for t in range(tiles)]))
                else:
                    terms.append(last)
        return expand(terms, moved, irows, kept)

    out = one_round(0)

    def more(state):
        r, total = state
        return r + 1, total + one_round(r * slots)

    return lax.while_loop(lambda s: s[0] < rounds, more, (jnp.int32(1), out))[1]


def solution(mesh):
    return jax.shard_map(
        local,
        mesh=mesh,
        in_specs=(
            P(("groups", "depth", "rep"), "tile"),
            P("groups", "tile"),
            P("groups"),
            P("groups"),
        ),
        out_specs=P(("groups", "tile"), ("depth", "rep")),
        check_vma=False,
    )
```

```python
import functools

import jax
import jax.numpy as jnp
from jax import lax
from jax.experimental import pallas as pl
from jax.experimental.pallas import tpu as pltpu
from jax.sharding import PartitionSpec as P

BF16, F32 = jnp.bfloat16, jnp.float32
def split(x):
    high = x.astype(BF16)
    return high, (x - high.astype(F32)).astype(BF16)


def merge_kernel(slots, rank_ref, irow_ref, col_ref, i_ref, y_ref, pick_ref):
    @pl.when(pl.program_id(0) == 0)
    def _():
        slot = lax.broadcasted_iota(jnp.int32, (slots, rank_ref.shape[1]), 0)
        pick_ref[...] = jnp.where(slot == rank_ref[...], 1.0, 0.0).T.astype(BF16)

    high, low = split(jnp.where(irow_ref[...] == col_ref[...], i_ref[...], 0.0))
    y_ref[:slots] = jnp.dot(high, pick_ref[...], preferred_element_type=F32).T.astype(BF16)
    y_ref[slots:] = jnp.dot(low, pick_ref[...], preferred_element_type=F32).T.astype(BF16)


def merge(integrals_t, rank, irows, cols, slots):
    depth, n = integrals_t.shape
    kb = 512
    padded = cols.shape[0]
    whole = lambda s: (0, 0)
    return pl.pallas_call(
        functools.partial(merge_kernel, slots),
        grid=(padded // kb,),
        out_shape=jax.ShapeDtypeStruct((2 * slots, padded), BF16),
        in_specs=[
            pl.BlockSpec((1, n), whole),
            pl.BlockSpec((1, n), whole),
            pl.BlockSpec((kb, 1), lambda s: (s, 0)),
            pl.BlockSpec((kb, n), lambda s: (jnp.minimum(s, (depth - 1) // kb), 0)),
        ],
        out_specs=pl.BlockSpec((2 * slots, kb), lambda s: (0, s)),
        scratch_shapes=[pltpu.VMEM((n, slots), BF16)],
        compiler_params=pltpu.CompilerParams(vmem_limit_bytes=40 * 1024 * 1024),
        cost_estimate=pl.CostEstimate(
            flops=4 * n * slots * depth, bytes_accessed=4 * (n + slots) * depth, transcendentals=0
        ),
    )(rank[None, :], irows[None, :], cols[:, None], integrals_t)


def chunk_kernel(slots, dest_ref, arow_ref, col_ref, a_ref, y_ref, z_ref):
    @pl.when(pl.program_id(0) == 0)
    def _():
        z_ref[...] = jnp.zeros_like(z_ref)

    a_high, a_low = split(jnp.where(arow_ref[...] == col_ref[...], a_ref[...], 0.0))
    both = jnp.dot(y_ref[...], a_high, preferred_element_type=F32)
    rest = jnp.dot(y_ref[:slots], a_low, preferred_element_type=F32)
    z_ref[...] += both[:slots] + both[slots:] + rest


def chunk(dest, amplitudes_t, y, arows, cols, width):
    depth, m = amplitudes_t.shape
    slots = y.shape[0] // 2
    kb = 1024 if width <= 1280 else 512
    return pl.pallas_call(
        functools.partial(chunk_kernel, slots),
        grid_spec=pltpu.PrefetchScalarGridSpec(
            num_scalar_prefetch=1,
            grid=(pl.cdiv(depth, kb),),
            in_specs=[
                pl.BlockSpec((1, width), lambda s, d: (0, d[0])),
                pl.BlockSpec((kb, 1), lambda s, d: (s, 0)),
                pl.BlockSpec((kb, width), lambda s, d: (s, d[0])),
                pl.BlockSpec((2 * slots, kb), lambda s, d: (0, s)),
            ],
            out_specs=pl.BlockSpec((slots, width), lambda s, d: (0, 0)),
        ),
        out_shape=jax.ShapeDtypeStruct((slots, width), F32),
        compiler_params=pltpu.CompilerParams(vmem_limit_bytes=52 * 1024 * 1024),
        cost_estimate=pl.CostEstimate(
            flops=6 * width * slots * depth, bytes_accessed=4 * (width + slots) * depth, transcendentals=0
        ),
    )(dest, arows[None, :], cols[:, None], amplitudes_t, y)


def expand_kernel(slots, rank_ref, icol_ref, row_ref, *refs):
    out_ref = refs[-1]
    slot = lax.broadcasted_iota(jnp.int32, (slots, rank_ref.shape[1]), 0)
    pick = jnp.where(slot == rank_ref[...], 1.0, 0.0).astype(BF16)
    total = refs[0][...]
    for z_ref in refs[1:-1]:
        total += z_ref[...]
    high, low = split(total.T)
    full = jnp.dot(high, pick, preferred_element_type=F32) + jnp.dot(low, pick, preferred_element_type=F32)
    out_ref[...] = jnp.where(row_ref[...] == icol_ref[...], full, 0.0)


def expand(terms, rank, irows, kept):
    slots, m = terms[0].shape
    n = rank.shape[0]
    block = 128 if m % 128 == 0 else m
    whole = lambda s: (0, 0)
    return pl.pallas_call(
        functools.partial(expand_kernel, slots),
        grid=(m // block,),
        out_shape=jax.ShapeDtypeStruct((m, n), F32),
        in_specs=[
            pl.BlockSpec((1, n), whole),
            pl.BlockSpec((1, n), whole),
            pl.BlockSpec((block, 1), lambda s: (s, 0)),
        ]
        + [pl.BlockSpec((slots, block), lambda s: (0, s))] * len(terms),
        out_specs=pl.BlockSpec((block, n), lambda s: (s, 0)),
        compiler_params=pltpu.CompilerParams(vmem_limit_bytes=32 * 1024 * 1024),
    )(rank[None, :], irows[None, :], kept[:, None], *terms)


def local(cycle_integrals, amplitudes, occupied_irreps, virtual_irreps):
    n, depth = cycle_integrals.shape
    m = amplitudes.shape[0]
    tiles = lax.axis_size("tile")
    occ = occupied_irreps.shape[0]
    reps = lax.axis_size("depth") * lax.axis_size("rep")
    used = -(-max(tiles * depth, m, reps * n) // occ)
    pair_irreps = jnp.bitwise_xor(virtual_irreps[:used, None], occupied_irreps[None, :]).reshape(-1)
    me = lax.axis_index("tile")
    cols = lax.dynamic_slice_in_dim(pair_irreps, me * depth, depth)
    cols = jnp.pad(cols, (0, -depth % 1024), constant_values=-1)
    row_start = (lax.axis_index("depth") * lax.axis_size("rep") + lax.axis_index("rep")) * n
    irows = lax.dynamic_slice_in_dim(pair_irreps, row_start, n)
    arows = pair_irreps[:m]
    kept_rows = m // tiles
    kept = lax.dynamic_slice_in_dim(arows, me * kept_rows, kept_rows)

    at = jnp.arange(n, dtype=jnp.int32)
    earlier = (irows[:, None] == irows[None, :]) & (at[:, None] < at[None, :])
    rank = jnp.sum(earlier.astype(jnp.int32), axis=0)
    slots = -(-3 * n // 1280) * 128

    every = pair_irreps[: reps * n].reshape(1, reps, n)
    counts = jnp.sum((every == jnp.arange(8, dtype=jnp.int32)[:, None, None]).astype(jnp.int32), axis=2)
    mine = jnp.broadcast_to(jnp.max(counts), (8, 128))
    most = mine
    groups = lax.axis_size("groups")
    for shift in range(1, groups):
        other = lax.ppermute(mine, "groups", [(g, (g + shift) % groups) for g in range(groups)])
        most = jnp.maximum(most, other)
    rounds = (most[0, 0] + slots - 1) // slots

    integrals_t, amplitudes_t = cycle_integrals.T, amplitudes.T

    def one_round(base):
        moved = rank - base
        y = merge(integrals_t, moved, irows, cols, slots)
        if tiles != 4 or kept_rows % 128:
            z = chunk(jnp.zeros((1,), jnp.int32), amplitudes_t, y, arows, cols, m)
            terms = [lax.psum_scatter(z, "tile", scatter_dimension=1, tiled=True)]
        else:
            side, place = me // 2, me % 2
            beside = [(t, t + 1 - 2 * (t % 2)) for t in range(4)]
            across = [(t, (t + 2) % 4) for t in range(4)]
            order = [(1 - side, 1 - place), (1 - side, place), (side, 1 - place), (side, place)]
            parts, last = [], None
            for to_side, to_place in order:
                dest = (2 * to_side + to_place).astype(jnp.int32).reshape(1)
                if last is not None:
                    dest, _ = lax.optimization_barrier((dest, last))
                last = chunk(dest, amplitudes_t, y, arows, cols, kept_rows)
                parts.append(last)
            gathered = parts[1] + lax.ppermute(parts[0], "tile", beside)
            terms = [
                parts[3],
                lax.ppermute(parts[2], "tile", beside),
                lax.ppermute(gathered, "tile", across),
            ]
        return expand(terms, moved, irows, kept)

    out = one_round(0)

    def more(state):
        r, total = state
        return r + 1, total + one_round(r * slots)

    return lax.while_loop(lambda s: s[0] < rounds, more, (jnp.int32(1), out))[1]


def solution(mesh):
    return jax.shard_map(
        local,
        mesh=mesh,
        in_specs=(
            P(("groups", "depth", "rep"), "tile"),
            P("groups", "tile"),
            P("groups"),
            P("groups"),
        ),
        out_specs=P(("groups", "tile"), ("depth", "rep")),
        check_vma=False,
    )
```
